128 devices in a mesh: grp: 4 (over z_hi, core), sub: 32 (over x, z_lo, y).
Axes of the slice: x: 4, y: 4, z: 4 (z_hi: 2, z_lo: 2; z = z_hi * 2 + z_lo), core: 2. Of those that a mesh axis runs over, the one named last changes fastest.
Arguments:
- left: bfloat16 [24576, 1536], P('sub', 'grp'), may hold values from -6 to 6
- right: bfloat16 [1536, 24576], P('sub', 'grp'), may hold values from -0.15625 to 0.15625
Outputs:
- product: bfloat16 [24576, 24576], P('sub', 'grp')
The draws below stay inside these ranges and needn't reach their ends.
All inputs are finite; a program needn't handle non-finite values.
Results may differ from the reference program's by a relative error of at most 0.001.
Values may be sent and summed in bfloat16 or wider, within the bound.
A program may use at most 128 MiB of HBM per device.

```python
import jax
import jax.numpy as jnp

M = 24576
N = 24576
K = 1536


def block_scale(stream_key, shape, shards, smallest, largest):
    level, own = 1.0, jax.random.fold_in(stream_key, 6)
    for axis_at, shards_of in shards:
        steps = jnp.exp(jax.random.uniform(jax.random.fold_in(own, axis_at), (shards_of,), jnp.float32, smallest / len(shards), largest / len(shards)))
        level = level * jnp.repeat(steps, shape[axis_at] // shards_of).reshape([-1 if axis == axis_at else 1 for axis in range(len(shape))])
    return level


def gaussian(own_key, dims, deviation, bound, shards=(), dtype=jnp.bfloat16):
    gain = block_scale(own_key, dims, shards, -0.22, 0.18) if shards else 1.0
    result = jax.random.normal(own_key, dims, jnp.float32) * deviation * gain
    return jnp.minimum(jnp.maximum(result, -bound), bound).astype(dtype)


def setup_inputs(seed: int = 0) -> dict:
    arg_keys = jax.random.split(jax.random.key(seed), 3)
    return {
        "left": gaussian(arg_keys[0], (M, K), 1.0, 6.0, ((0, 32), (1, 4))),
        "right": gaussian(arg_keys[1], (K, N), K ** -0.5, 0.15625, ((0, 32), (1, 4))),
    }


def reference(left, right):
    full_sum = jnp.dot(left, right, preferred_element_type=jnp.float32)
    return full_sum.astype(jnp.bfloat16)
```

```python
import functools

import jax
import jax.numpy as jnp
from jax import lax
from jax.experimental import pallas as pl
from jax.experimental.pallas import tpu as pltpu
from jax.sharding import PartitionSpec as P

MESH = pl.DeviceIdType.MESH
M, N, K, DEPTH, KL = 768, 6144, 1536, 48, 384
W = 256
NS = 5
ND = N // W - 2 * NS
NC = NS + ND
TILE = 256
OWN, MATE = 0, 1


def kernel(left, right, out, held, rows, theirs, recv, send, lrecv, lsend, orecv, osend, local):
    grp, sub = lax.axis_index("grp"), lax.axis_index("sub")
    zh, core = grp // 2, lax.rem(grp, 2)
    x, zl, y = sub // 8, lax.rem(sub // 4, 2), lax.rem(sub, 4)

    def device(x, y, zh, zl, core):
        return (zh * 2 + core, x * 8 + zl * 4 + y)

    xr, xl, yr, yl = lax.rem(x + 1, 4), lax.rem(x + 3, 4), lax.rem(y + 1, 4), lax.rem(y + 3, 4)
    x_right, x_left = device(xr, y, zh, zl, core), device(xl, y, zh, zl, core)
    y_right, y_left = device(x, yr, zh, zl, core), device(x, yl, zh, zl, core)
    mate = device(x, y, zh, 1 - zl, core)
    cross = device(x, y, 1 - zh, 1 - zl, core)
    sibling = device(x, y, zh, zl, 1 - core)
    around = (x_right, x_left, y_right, y_left, mate, cross, sibling)

    barrier = pltpu.get_barrier_semaphore()
    for other in around:
        pl.semaphore_signal(barrier, inc=1, device_id=other, device_id_type=MESH)

    def column(i, side):
        if i < NS:
            return pl.multiple_of(side * (NS * W) + i * W, 128)
        return (NS + i) * W

    def go(src, dst, ssem, rsem, to):
        copy = pltpu.make_async_remote_copy(src, dst, ssem, rsem, device_id=to, device_id_type=MESH)
        copy.start()
        return copy

    own = []
    for i in range(NC):
        copy = pltpu.make_async_copy(right.at[:, pl.ds(column(i, zl), W)], held.at[i, x, zl, y], local.at[i])
        copy.start()
        own.append(copy)
    mine = pltpu.make_async_copy(left, rows.at[OWN, :, pl.ds(pl.multiple_of(grp * KL, 128), KL)], local.at[NC])
    mine.start()
    pl.semaphore_wait(barrier, len(around))

    sent = []
    started = {}

    for i in range(NC):
        started[i, 0] = (go(right.at[:, pl.ds(column(i, 1 - zl), W)], held.at[i, x, zl, y], send.at[i, 0], recv.at[i, 0], mate),)

    def kcols(g):
        return pl.ds(pl.multiple_of(g * KL, 128), KL)

    other = (1 - zh) * 2 + core
    lcopy = {}
    lcopy["z"] = go(left, rows.at[MATE, :, kcols(grp)], lsend.at[0], lrecv.at[0], mate)
    lcopy["c"] = go(left, rows.at[MATE, :, kcols(grp)], lsend.at[1], lrecv.at[1], cross)
    lcopy["s0"] = go(left, rows.at[OWN, :, kcols(grp)], lsend.at[2], lrecv.at[2], sibling)

    def left_mate():
        lcopy["z"].wait_recv()
        block = rows.at[MATE, :, kcols(grp)]
        lcopy["c2"] = go(block, rows.at[OWN, :, kcols(grp)], lsend.at[3], lrecv.at[3], cross)
        lcopy["s1"] = go(block, block, lsend.at[4], lrecv.at[4], sibling)
        lcopy["c"].wait_recv()
        block = rows.at[MATE, :, kcols(other)]
        lcopy["s2"] = go(block, block, lsend.at[5], lrecv.at[5], sibling)

    def left_own():
        lcopy["c2"].wait_recv()
        block = rows.at[OWN, :, kcols(other)]
        lcopy["s3"] = go(block, block, lsend.at[6], lrecv.at[6], sibling)
        lcopy["s0"].wait_recv()
        mine.wait()

    def piece(i, along, a, b, z):
        return held.at[i, a, z, b] if along == 0 else held.at[i, b, z, a]

    def stage(i, k):
        first = i % 2
        if k in (1, 2):
            along = first
        else:
            along = 1 - first
        here, lo, hi = ((x, xl, xr), (y, yl, yr))[along]
        fixed = (y, x)[along] if k in (1, 2) else slice(None)
        right_to, left_to = ((x_right, x_left), (y_right, y_left))[along]
        for copy in started[i, k - 1]:
            copy.wait_recv()
        if k == 1:
            own[i].wait()
        if k in (1, 3):
            up = down = piece(i, along, here, fixed, slice(None))
        else:
            up, down = piece(i, along, lo, fixed, 0), piece(i, along, hi, fixed, 1)
        s, r = send.at[i], recv.at[i]
        started[i, k] = (
            go(up, up, s.at[2 * k - 1], r.at[2 * k - 1], right_to),
            go(down, down, s.at[2 * k], r.at[2 * k], left_to),
        )

    def multiply(side, i, write):
        block = held.at[i]

        @pl.loop(0, M // TILE)
        def _(t):
            at = pl.ds(pl.multiple_of(t * TILE, TILE), TILE)
            value = jnp.dot(rows[side, at, :], block[...].reshape(K, W), preferred_element_type=jnp.float32)
            write(at, value.astype(jnp.bfloat16))

    outs = []

    def compute_mate(i):
        def write(at, value):
            theirs[i, at, :] = value

        multiply(MATE, i, write)
        c = column(i, zl)
        outs.append(go(theirs.at[i], out.at[:, pl.ds(c, W)], osend.at[i], orecv.at[i], mate))

    def compute_own(i):
        c = column(i, zl)

        def write(at, value):
            out[at, pl.ds(c, W)] = value

        multiply(OWN, i, write)

    ready = []
    mates = own_ready = False
    for t in range(NC + LAG[5] + 1):
        for k in (4, 3, 2, 1):
            for i in range(NC):
                if t == max(i - AHEAD, 0) + LAG[k] if k < 3 else t == i + LAG[k]:
                    stage(i, k)
        if t == LEFT_MATE:
            left_mate()
        if t == LEFT_OWN:
            left_own()
            lcopy["s3"].wait_recv()
            own_ready = True
        i = t - LAG[5]
        if 0 <= i < NC:
            for copy in started[i, 4]:
                copy.wait_recv()
            if i < NS:
                if not mates:
                    lcopy["s1"].wait_recv()
                    lcopy["s2"].wait_recv()
                    mates = True
                compute_mate(i)
            ready.append(i)
        if own_ready:
            for _ in range(2):
                if ready:
                    compute_own(ready.pop(0))
    while ready:
        compute_own(ready.pop(0))

    for copies in started.values():
        for copy in copies:
            copy.wait_send()
    for copy in lcopy.values():
        copy.wait_send()
    for copy in outs:
        copy.wait()


LAG = [0, 0, 1, 2, 4, 6]
AHEAD = 4
LEFT_MATE, LEFT_OWN = 4, 8


def shards(left, right):
    flops = 2 * M * N * K
    return pl.pallas_call(
        kernel,
        out_shape=OUT,
        in_specs=[pl.BlockSpec(memory_space=pl.ANY)] * 2,
        out_specs=pl.BlockSpec(memory_space=pltpu.VMEM),
        scratch_shapes=[
            pltpu.VMEM((NC, 4, 2, 4, DEPTH, W), jnp.bfloat16),
            pltpu.VMEM((2, M, K), jnp.bfloat16),
            pltpu.VMEM((NS, M, W), jnp.bfloat16),
            pltpu.SemaphoreType.DMA((NC, 9)),
            pltpu.SemaphoreType.DMA((NC, 9)),
            pltpu.SemaphoreType.DMA((7,)),
            pltpu.SemaphoreType.DMA((7,)),
            pltpu.SemaphoreType.DMA((NS,)),
            pltpu.SemaphoreType.DMA((NS,)),
            pltpu.SemaphoreType.DMA((NC + 1,)),
        ],
        compiler_params=pltpu.CompilerParams(
            collective_id=0, has_side_effects=True, vmem_limit_bytes=50 * 2**20
        ),
        cost_estimate=pl.CostEstimate(flops=flops, bytes_accessed=2 * M * N, transcendentals=0),
    )(left, right)


OUT = jax.ShapeDtypeStruct((M, N), jnp.bfloat16)


def solution(mesh):
    placed = (P("sub", "grp"), P("sub", "grp"))
    return jax.shard_map(
        shards, mesh=mesh, in_specs=placed, out_specs=P("sub", "grp"), check_vma=False
    )
```

```python
import jax
import jax.numpy as jnp
from jax import lax
from jax.experimental import pallas as pl
from jax.experimental.pallas import tpu as pltpu
from jax.sharding import PartitionSpec as P

MESH = pl.DeviceIdType.MESH
M, N, K, DEPTH, KL = 768, 6144, 1536, 48, 384
W = 256
NS = 6
ND = N // W - 2 * NS
NC = NS + ND
TILE = 256
OWN, MATE = 0, 1

ORDER = (
    ("z", 1), ("z", 0), ("z", 13), ("z", 2), ("z", 3), ("z", 5), ("z", 10), ("z", 9),
    ("z", 4), (1, 1), (1, 0), (1, 13), ("z", 11), ("L", 0), (1, 2), ("z", 12),
    (1, 3), (1, 10), (1, 5), (2, 1), (2, 0), ("z", 6), (1, 11), (1, 9),
    ("z", 15), ("z", 8), (2, 2), (1, 4), (2, 13), (2, 3), (2, 10), (3, 1),
    (3, 0), (3, 2), (3, 3), ("z", 14), (2, 4), (4, 1), (2, 11), (2, 5),
    ("LM", 0), ("z", 17), (4, 0), (1, 6), ("z", 7), ("z", 16), (4, 2), (1, 14),
    (1, 15), (4, 3), (2, 9), (3, 4), (1, 16), (1, 8), ("m", 1), (1, 12),
    (3, 10), ("m", 2), (2, 14), (2, 6), (2, 16), (1, 17), (1, 7), (3, 13),
    (3, 14), (3, 5), (3, 9), ("LO", 0), (4, 10), (2, 15), (4, 13), (4, 5),
    (2, 17), (2, 7), (2, 8), (2, 12), (3, 16), ("m", 0), (4, 9), ("m", 3),
    (3, 15), (4, 14), (3, 11), (3, 6), (4, 16), ("o", 3), ("o", 1), (4, 4),
    (3, 12), (3, 8), ("m", 5), (3, 7), ("o", 14), ("o", 0), ("o", 13), ("o", 9),
    (4, 6), ("o", 10), (4, 15), ("o", 2), ("m", 4), (3, 17), ("o", 5), ("o", 4),
    ("o", 16), (4, 7), (4, 12), ("o", 15), (4, 8), (4, 11), ("o", 6), (4, 17),
    ("o", 7), ("o", 12), ("o", 8), ("o", 11), ("o", 17),
)


def kernel(left, right, out, held, rows, theirs, zrecv, recv, send, lrecv, lsend, osem, local):
    grp, sub = lax.axis_index("grp"), lax.axis_index("sub")
    zh, core = grp // 2, lax.rem(grp, 2)
    x, zl, y = sub // 8, lax.rem(sub // 4, 2), lax.rem(sub, 4)

    def device(x, y, zh, zl, core):
        return (zh * 2 + core, x * 8 + zl * 4 + y)

    xr, xl, yr, yl = lax.rem(x + 1, 4), lax.rem(x + 3, 4), lax.rem(y + 1, 4), lax.rem(y + 3, 4)
    x_right, x_left = device(xr, y, zh, zl, core), device(xl, y, zh, zl, core)
    y_right, y_left = device(x, yr, zh, zl, core), device(x, yl, zh, zl, core)
    mate = device(x, y, zh, 1 - zl, core)
    cross = device(x, y, 1 - zh, 1 - zl, core)
    sibling = device(x, y, zh, zl, 1 - core)
    around = (x_right, x_left, y_right, y_left, mate, cross, sibling)

    barrier = pltpu.get_barrier_semaphore()
    for other in around:
        pl.semaphore_signal(barrier, inc=1, device_id=other, device_id_type=MESH)

    def column(i, side):
        if i < NS:
            return pl.multiple_of(side * (NS * W) + i * W, 128)
        return (NS + i) * W

    def kcols(g):
        return pl.ds(pl.multiple_of(g * KL, 128), KL)

    def go(src, dst, ssem, rsem, to):
        pltpu.make_async_remote_copy(src, dst, ssem, rsem, device_id=to, device_id_type=MESH).start()

    def wait(like, sem):
        pltpu.make_async_copy(like, like, sem).wait()

    for i in range(NC):
        pltpu.make_async_copy(right.at[:, pl.ds(column(i, zl), W)], held.at[i, x, zl, y], local.at[0]).start()
    mine = pltpu.make_async_copy(left, rows.at[OWN, :, kcols(grp)], local.at[1])
    mine.start()
    with jax.named_scope("barrier"):
        pl.semaphore_wait(barrier, len(around))

    here_k, other_k = kcols(grp), kcols((1 - zh) * 2 + core)
    a_block = rows.at[0, :, pl.ds(0, KL)]
    two_blocks, three_blocks = rows.at[0, :, pl.ds(0, 2 * KL)], rows.at[0, :, pl.ds(0, 3 * KL)]

    def exchange(i):
        src = right.at[:, pl.ds(column(i, 1 - zl), W)]
        go(src, held.at[i, x, zl, y], send.at[0], zrecv.at[i], mate)

    def left_first():
        go(left, rows.at[MATE, :, here_k], lsend.at[0], lrecv.at[0], mate)
        go(left, rows.at[MATE, :, here_k], lsend.at[0], lrecv.at[1], cross)
        go(left, rows.at[OWN, :, here_k], lsend.at[0], lrecv.at[4], sibling)

    def left_mate():
        wait(a_block, lrecv.at[0])
        block = rows.at[MATE, :, here_k]
        go(block, rows.at[OWN, :, here_k], lsend.at[0], lrecv.at[2], cross)
        go(block, block, lsend.at[1], lrecv.at[3], sibling)
        wait(a_block, lrecv.at[1])
        block = rows.at[MATE, :, other_k]
        go(block, block, lsend.at[1], lrecv.at[3], sibling)

    def left_own():
        wait(a_block, lrecv.at[2])
        block = rows.at[OWN, :, other_k]
        go(block, block, lsend.at[1], lrecv.at[4], sibling)
        mine.wait()

    def arrived(i, k):
        like = (None, held.at[i, 0, 0], held.at[i, 0, :, 0], held.at[i, :, 0], held.at[i, 0])[k]
        wait(like, recv.at[i, k - 1])

    def piece(i, along, a, b, z):
        return held.at[i, a, z, b] if along == 0 else held.at[i, b, z, a]

    def stage(i, k):
        first = i % 2
        along = first if k < 3 else 1 - first
        here, lo, hi = ((x, xl, xr), (y, yl, yr))[along]
        fixed = (y, x)[along] if k < 3 else slice(None)
        right_to, left_to = ((x_right, x_left), (y_right, y_left))[along]
        if k == 1:
            wait(held.at[i, 0, 0, 0], zrecv.at[i])
        else:
            arrived(i, k - 1)
        if k in (1, 3):
            up = down = piece(i, along, here, fixed, slice(None))
        else:
            up, down = piece(i, along, lo, fixed, 0), piece(i, along, hi, fixed, 1)
        go(up, up, send.at[k], recv.at[i, k - 1], right_to)
        go(down, down, send.at[k], recv.at[i, k - 1], left_to)

    def multiply(side, i, write):
        block = held.at[i]

        @pl.loop(0, M // TILE)
        def _(t):
            at = pl.ds(pl.multiple_of(t * TILE, TILE), TILE)
            value = jnp.dot(rows[side, at, :], block[...].reshape(K, W), preferred_element_type=jnp.float32)
            write(at, value.astype(jnp.bfloat16))

    def compute_mate(i):
        def write(at, value):
            theirs[i, at, :] = value

        multiply(MATE, i, write)
        go(theirs.at[i], out.at[:, pl.ds(column(i, zl), W)], osem.at[0], osem.at[1], mate)

    def compute_own(i):
        c = column(i, zl)

        def write(at, value):
            out[at, pl.ds(c, W)] = value

        multiply(OWN, i, write)

    met = set()

    def once(what):
        new = what not in met
        met.add(what)
        return new

    def full(i):
        if once(("full", i)):
            with jax.named_scope(f"w4_{i}"):
                arrived(i, 4)

    for op, i in ORDER:
        if op == 1 and once("local"):
            wait(held.at[:, 0, 0, 0], local.at[0])
        if op in ("m", "o"):
            full(i)
        if op == "m" and once("mate"):
            with jax.named_scope("wmate"):
                wait(two_blocks, lrecv.at[3])
        if op == "o" and once("own"):
            with jax.named_scope("wown"):
                wait(two_blocks, lrecv.at[4])
        with jax.named_scope(f"{op}_{i}"):
            if op == "z":
                exchange(i)
            elif op == "L":
                left_first()
            elif op == "LM":
                left_mate()
            elif op == "LO":
                left_own()
            elif op == "m":
                compute_mate(i)
            elif op == "o":
                compute_own(i)
            else:
                stage(i, op)

    with jax.named_scope("sends"):
        for k, like in enumerate(
            (held.at[:, 0, 0, 0], held.at[:, 0, 0], held.at[:, 0, :, 0], held.at[:, :, 0], held.at[:, 0])
        ):
            wait(like, send.at[k])
        wait(rows.at[0], lsend.at[0])
        wait(three_blocks, lsend.at[1])
    with jax.named_scope("outs"):
        wait(theirs, osem.at[0])
        wait(theirs, osem.at[1])


def shards(left, right):
    return pl.pallas_call(
        kernel,
        out_shape=pltpu.VMEM((M, N), jnp.bfloat16),
        in_specs=[pl.BlockSpec(memory_space=pltpu.HBM)] * 2,
        out_specs=pl.BlockSpec(memory_space=pltpu.VMEM),
        scratch_shapes=[
            pltpu.VMEM((NC, 4, 2, 4, DEPTH, W), jnp.bfloat16),
            pltpu.VMEM((2, M, K), jnp.bfloat16),
            pltpu.VMEM((NS, M, W), jnp.bfloat16),
            pltpu.SemaphoreType.DMA((NC,)),
            pltpu.SemaphoreType.DMA((NC, 4)),
            pltpu.SemaphoreType.DMA((5,)),
            pltpu.SemaphoreType.DMA((5,)),
            pltpu.SemaphoreType.DMA((2,)),
            pltpu.SemaphoreType.DMA((2,)),
            pltpu.SemaphoreType.DMA((2,)),
        ],
        compiler_params=pltpu.CompilerParams(
            collective_id=0, has_side_effects=True, vmem_limit_bytes=50 * 2**20
        ),
        cost_estimate=pl.CostEstimate(flops=2 * M * N * K, bytes_accessed=2 * M * N, transcendentals=0),
    )(left, right)


def solution(mesh):
    placed = (P("sub", "grp"), P("sub", "grp"))
    return jax.shard_map(
        shards, mesh=mesh, in_specs=placed, out_specs=P("sub", "grp"), check_vma=False
    )
```

```python
import jax
import jax.numpy as jnp
from jax import lax
from jax.experimental import pallas as pl
from jax.experimental.pallas import tpu as pltpu
from jax.sharding import PartitionSpec as P

MESH = pl.DeviceIdType.MESH
M, N, K, DEPTH, KL = 768, 6144, 1536, 48, 384
W = 256
NS = 6
ND = N // W - 2 * NS
NC = NS + ND
LAST = 2
NA = N - LAST * W
TILE = 256
PARTS = 3
OWN, MATE = 0, 1

ORDER = (
    ("z", 4), ("z", 1), ("p", 17), ("p", 10), ("z", 2), ("z", 5), ("p", 13), ("z", 15),
    ("p", 6), ("p", 16), ("p", 4), ("p", 12), ("p", 15), ("p", 11), ("z", 10), ("p", 0),
    ("p", 1), ("z", 0), ("L", 1), (1, 4), ("L", 2), ("p", 14), ("p", 2), (1, 1),
    ("p", 9), (1, 2), (1, 5), ("L", 0), (1, 15), ("p", 5), ("z", 3), (2, 4),
    (2, 1), ("p", 7), (2, 15), ("z", 11), (1, 10), ("z", 8), ("z", 17), ("p", 8),
    (2, 2), ("p", 3), ("z", 9), (1, 0), ("z", 14), ("z", 6), ("z", 16), (2, 5),
    ("z", 13), (3, 4), (3, 1), ("LM", 1), (3, 2), (2, 10), ("LM", 2), (2, 0),
    (4, 4), (4, 1), (3, 15), ("LM", 0), (1, 11), (4, 2), ("LO", 1), (1, 17),
    ("z", 7), (1, 14), (3, 0), (3, 5), ("z", 12), ("m", 1), (2, 11), (1, 12),
    (1, 8), (4, 15), ("m", 4), (1, 7), (2, 17), (1, 16), (4, 0), (1, 6),
    (1, 13), (2, 14), (3, 11), (2, 7), (1, 3), (2, 12), (3, 10), (4, 5),
    (2, 8), ("m", 0), (1, 9), ("m", 2), (2, 16), (2, 3), (4, 10), (2, 13),
    (2, 6), (3, 7), (2, 9), (3, 12), ("LO", 0), ("m", 5), (3, 3), (3, 14),
    ("LO", 2), (4, 7), (4, 11), (3, 6), (4, 3), ("o", 15), (3, 8), ("o", 4),
    (3, 9), ("o", 0), ("o", 1), (4, 14), (4, 6), ("o", 10), (3, 16), (3, 13),
    ("o", 11), (4, 9), (3, 17), ("m", 3), (4, 12), (4, 8), ("o", 2), ("o", 7),
    ("o", 5), ("o", 14), ("o", 3), (4, 13), ("o", 6), (4, 16), ("o", 9), (4, 17),
    ("o", 12), ("o", 8), ("o", 13), ("f", 16), ("f", 17),
)


def gather(left, right, out, own, tail, held, others, theirs, zrecv, recv, send, lrecv, lsend, sibrecv, osem, local):
    grp, sub = lax.axis_index("grp"), lax.axis_index("sub")
    zh, core = grp // 2, lax.rem(grp, 2)
    x, zl, y = sub // 8, lax.rem(sub // 4, 2), lax.rem(sub, 4)

    def device(x, y, zh, zl, core):
        return (zh * 2 + core, x * 8 + zl * 4 + y)

    xr, xl, yr, yl = lax.rem(x + 1, 4), lax.rem(x + 3, 4), lax.rem(y + 1, 4), lax.rem(y + 3, 4)
    x_right, x_left = device(xr, y, zh, zl, core), device(xl, y, zh, zl, core)
    y_right, y_left = device(x, yr, zh, zl, core), device(x, yl, zh, zl, core)
    mate = device(x, y, zh, 1 - zl, core)
    cross = device(x, y, 1 - zh, 1 - zl, core)
    sibling = device(x, y, zh, zl, 1 - core)
    around = (x_right, x_left, y_right, y_left, mate, cross, sibling)

    rows = (own, others)

    def chunk(i):
        return held.at[i] if i < NC - LAST else tail.at[i - (NC - LAST)]

    barrier = pltpu.get_barrier_semaphore()
    for other in around:
        pl.semaphore_signal(barrier, inc=1, device_id=other, device_id_type=MESH)

    def column(i, side):
        if i < NS:
            return pl.multiple_of(side * (NS * W) + i * W, 128)
        return (NS + i) * W

    def kcols(g):
        return pl.ds(pl.multiple_of(g * KL, 128), KL)

    def go(src, dst, ssem, rsem, to):
        pltpu.make_async_remote_copy(src, dst, ssem, rsem, device_id=to, device_id_type=MESH).start()

    def wait(like, sem):
        pltpu.make_async_copy(like, like, sem).wait()

    for i in range(NC):
        pltpu.make_async_copy(right.at[:, pl.ds(column(i, zl), W)], chunk(i).at[x, zl, y], local.at[0]).start()
    mine = pltpu.make_async_copy(left, own.at[:, kcols(grp)], local.at[1])
    mine.start()
    with jax.named_scope("barrier"):
        pl.semaphore_wait(barrier, len(around))

    here_k, other_k = kcols(grp), kcols((1 - zh) * 2 + core)
    some = NC // 2
    a_part = own.at[pl.ds(0, M // PARTS), pl.ds(0, KL)]
    two_blocks, three_blocks = own.at[:, pl.ds(0, 2 * KL)], own.at[:, pl.ds(0, 3 * KL)]

    def exchange(i):
        src = right.at[:, pl.ds(column(i, 1 - zl), W)]
        go(src, chunk(i).at[x, zl, y], send.at[0], zrecv.at[i], mate)

    def part(j):
        return pl.ds(j * (M // PARTS), M // PARTS)

    def left_first(j):
        go(left.at[part(j)], others.at[part(j), here_k], lsend.at[0], lrecv.at[0, j], mate)
        go(left.at[part(j)], others.at[part(j), here_k], lsend.at[0], lrecv.at[1, j], cross)
        go(left.at[part(j)], own.at[part(j), here_k], lsend.at[0], sibrecv.at[1], sibling)

    def left_mate(j):
        wait(a_part, lrecv.at[0, j])
        block = others.at[part(j), here_k]
        go(block, own.at[part(j), here_k], lsend.at[0], lrecv.at[2, j], cross)
        go(block, block, lsend.at[1], sibrecv.at[0], sibling)
        wait(a_part, lrecv.at[1, j])
        block = others.at[part(j), other_k]
        go(block, block, lsend.at[1], sibrecv.at[0], sibling)

    def left_own(j):
        wait(a_part, lrecv.at[2, j])
        block = own.at[part(j), other_k]
        go(block, block, lsend.at[1], sibrecv.at[1], sibling)

    def arrived(i, k):
        like = (None, held.at[0, 0, 0], held.at[0, 0, :, 0], held.at[0, 0], held.at[0, :, 0])[k]
        wait(like, recv.at[i, k - 1])

    def piece(i, along, a, b, z):
        return chunk(i).at[a, z, b] if along == 0 else chunk(i).at[b, z, a]

    def both(i, k, up, down, to):
        go(up, up, send.at[k], recv.at[i, k - 1], to[0])
        go(down, down, send.at[k], recv.at[i, k - 1], to[1])

    def stage(i, k):
        first = i % 2
        along = first if k < 3 else 1 - first
        here, lo, hi = ((x, xl, xr), (y, yl, yr))[along]
        fixed = (y, x)[along] if k < 3 else slice(None)
        to = ((x_right, x_left), (y_right, y_left))[along]
        if k == 0:
            src, dst = right.at[:, pl.ds(column(i, zl), W)], chunk(i).at[x, zl, y]
            go(src, dst, send.at[1], recv.at[i, 0], to[0])
            go(src, dst, send.at[1], recv.at[i, 0], to[1])
        elif k == 1:
            wait(held.at[0, 0, 0, 0], zrecv.at[i])
            block = chunk(i).at[x, 1 - zl, y]
            both(i, 1, block, block, to)
        else:
            arrived(i, k - 1)
            if k == 3:
                low, high = piece(i, along, here, fixed, 0), piece(i, along, here, fixed, 1)
                both(i, 3, low, high, to)
                go(high, high, send.at[3], recv.at[i, 3], to[0])
                go(low, low, send.at[3], recv.at[i, 3], to[1])
            else:
                both(i, k, piece(i, along, lo, fixed, 0), piece(i, along, hi, fixed, 1), to)

    def multiply(side, i, write):
        block = chunk(i)

        @pl.loop(0, M // TILE)
        def _(t):
            at = pl.ds(pl.multiple_of(t * TILE, TILE), TILE)
            value = jnp.dot(rows[side][at, :], block[...].reshape(K, W), preferred_element_type=jnp.float32)
            write(at, value.astype(jnp.bfloat16))

    def compute_mate(i):
        def write(at, value):
            theirs[i, at, :] = value

        multiply(MATE, i, write)
        go(theirs.at[i], out.at[:, pl.ds(column(i, zl), W)], osem.at[0], osem.at[1], mate)

    def compute_own(i):
        c = column(i, zl)

        def write(at, value):
            out[at, pl.ds(c, W)] = value

        multiply(OWN, i, write)

    met = set()

    def once(what):
        new = what not in met
        met.add(what)
        return new

    def full(i):
        if once(("full", i)):
            with jax.named_scope(f"w4_{i}"):
                arrived(i, 4)

    for op, i in ORDER:
        if op == 3 and once("local"):
            wait(held.at[pl.ds(0, some), 0, :, 0], local.at[0])
        if op in ("m", "o", "f"):
            full(i)
        if op == "m" and once("mate"):
            with jax.named_scope("wmate"):
                wait(two_blocks, sibrecv.at[0])
        if op == "o" and once("own"):
            with jax.named_scope("wown"):
                wait(two_blocks, sibrecv.at[1])
                mine.wait()
        with jax.named_scope(f"{op}_{i}"):
            if op == "z":
                exchange(i)
            elif op == "p":
                stage(i, 0)
            elif op == "L":
                left_first(i)
            elif op == "LM":
                left_mate(i)
            elif op == "LO":
                left_own(i)
            elif op == "m":
                compute_mate(i)
            elif op == "o":
                compute_own(i)
            elif op != "f":
                stage(i, op)

    with jax.named_scope("sends"):
        for k, like in enumerate((
            held.at[pl.ds(0, some), 0, :, 0],
            held.at[pl.ds(0, some), 0],
            held.at[pl.ds(0, some), 0, 0],
            held.at[pl.ds(0, some)],
            held.at[pl.ds(0, some), :, 0],
        )):
            wait(like, send.at[k])
        wait(own, lsend.at[0])
        wait(three_blocks, lsend.at[1])
    with jax.named_scope("outs"):
        wait(theirs, osem.at[0])
        wait(theirs, osem.at[1])


def finish(done, own, tail, out, last, sems):
    copies = []
    for b in range(BLOCKS):
        at = pl.ds(b * (M // BLOCKS), M // BLOCKS)
        copies.append(pltpu.make_async_copy(done.at[at], out.at[at, pl.ds(0, NA)], sems.at[b]))
        copies[-1].start()
    for j in range(LAST):

        @pl.loop(0, M // TILE)
        def _(t):
            at = pl.ds(pl.multiple_of(t * TILE, TILE), TILE)
            value = jnp.dot(own[at, :], tail[j].reshape(K, W), preferred_element_type=jnp.float32)
            last[j, at, :] = value.astype(jnp.bfloat16)

        copies.append(pltpu.make_async_copy(last.at[j], out.at[:, pl.ds(NA + j * W, W)], sems.at[BLOCKS + j]))
        copies[-1].start()
    for copy in copies:
        copy.wait()


BLOCKS = 4


def shards(left, right):
    chunks = (4, 2, 4, DEPTH, W)
    done, own, tail = pl.pallas_call(
        gather,
        out_shape=(
            pltpu.VMEM((M, NA), jnp.bfloat16),
            pltpu.VMEM((M, K), jnp.bfloat16),
            pltpu.VMEM((LAST,) + chunks, jnp.bfloat16),
        ),
        in_specs=[pl.BlockSpec(memory_space=pltpu.HBM)] * 2,
        out_specs=(pl.BlockSpec(memory_space=pltpu.VMEM),) * 3,
        scratch_shapes=[
            pltpu.VMEM((NC - LAST,) + chunks, jnp.bfloat16),
            pltpu.VMEM((M, K), jnp.bfloat16),
            pltpu.VMEM((NS, M, W), jnp.bfloat16),
            pltpu.SemaphoreType.DMA((NC,)),
            pltpu.SemaphoreType.DMA((NC, 4)),
            pltpu.SemaphoreType.DMA((5,)),
            pltpu.SemaphoreType.DMA((3, PARTS)),
            pltpu.SemaphoreType.DMA((2,)),
            pltpu.SemaphoreType.DMA((2,)),
            pltpu.SemaphoreType.DMA((2,)),
            pltpu.SemaphoreType.DMA((2,)),
        ],
        compiler_params=pltpu.CompilerParams(
            collective_id=0, has_side_effects=True, vmem_limit_bytes=GRANT
        ),
        cost_estimate=pl.CostEstimate(flops=2 * M * NA * K, bytes_accessed=2 * M * N, transcendentals=0),
    )(left, right)
    return pl.pallas_call(
        finish,
        out_shape=jax.ShapeDtypeStruct((M, N), jnp.bfloat16),
        in_specs=[pl.BlockSpec(memory_space=pltpu.VMEM)] * 3,
        out_specs=pl.BlockSpec(memory_space=pltpu.HBM),
        scratch_shapes=[pltpu.VMEM((LAST, M, W), jnp.bfloat16), pltpu.SemaphoreType.DMA((BLOCKS + LAST,))],
        compiler_params=pltpu.CompilerParams(vmem_limit_bytes=16 * 2**20),
        cost_estimate=pl.CostEstimate(flops=2 * M * LAST * W * K, bytes_accessed=4 * M * N, transcendentals=0),
    )(done, own, tail)


GRANT = 48 * 2**20


def solution(mesh):
    placed = (P("sub", "grp"), P("sub", "grp"))
    return jax.shard_map(
        shards, mesh=mesh, in_specs=placed, out_specs=P("sub", "grp"), check_vma=False
    )
```

```python
import jax
import jax.numpy as jnp
from jax import lax
from jax.experimental import pallas as pl
from jax.experimental.pallas import tpu as pltpu
from jax.sharding import PartitionSpec as P

MESH = pl.DeviceIdType.MESH
M, N, K, DEPTH, KL = 768, 6144, 1536, 48, 384
W = 256
NS = 6
ND = N // W - 2 * NS
NC = NS + ND
LAST = 2
NA = N - LAST * W
TILE = 256
PARTS = 3
OWN, MATE = 0, 1

ORDER = (
    ("z", 4), ("z", 1), ("z", 9), ("p", 4), ("p", 9), ("z", 12), ("z", 5), ("p", 14),
    ("z", 3), ("p", 15), ("z", 16), ("p", 13), ("z", 15), ("p", 11), ("p", 2), ("z", 14),
    ("p", 1), ("z", 2), ("z", 0), ("L", 1), ("p", 10), ("L", 0), ("L", 2), (1, 4),
    (1, 1), ("p", 0), (1, 9), (1, 12), ("z", 6), ("p", 12), (1, 5), ("p", 5),
    ("p", 16), ("z", 13), ("p", 7), (1, 16), (1, 15), (2, 4), ("p", 8), ("z", 11),
    (1, 14), ("p", 6), (2, 1), ("z", 10), ("p", 17), (1, 0), ("p", 3), (1, 3),
    (2, 5), (1, 2), (2, 12), (2, 9), ("z", 7), (2, 16), (3, 4), (3, 1),
    (2, 15), (2, 3), (2, 2), (2, 14), ("LM", 1), (4, 4), (3, 5), (4, 1),
    (3, 12), ("LM", 0), ("z", 17), ("LM", 2), ("z", 8), (3, 2), (3, 3), (2, 0),
    (1, 11), (1, 6), (3, 14), (3, 9), ("m", 4), (4, 5), (4, 3), (1, 10),
    (1, 7), (4, 12), (1, 8), ("m", 1), (3, 0), ("LO", 2), ("LO", 0), (3, 15),
    ("LO", 1), (1, 13), (1, 17), (2, 7), (2, 11), (4, 2), ("m", 3), (4, 14),
    (2, 8), (2, 6), (4, 0), (4, 9), (3, 7), (3, 6), (2, 13), (3, 11),
    (2, 17), ("m", 2), ("m", 0), ("m", 5), (3, 8), (4, 15), (2, 10), ("o", 2),
    (4, 6), ("o", 9), ("o", 0), (3, 13), ("o", 5), (4, 11), ("o", 3), ("o", 14),
    (4, 7), (4, 8), (3, 10), (3, 16), (3, 17), ("o", 12), ("o", 1), (4, 13),
    ("o", 4), (4, 10), ("o", 11), ("o", 8), ("o", 15), ("o", 6), (4, 17), (4, 16),
    ("o", 7), ("o", 10), ("o", 13), ("f", 17), ("f", 16),
)


def gather(left, right, out, own, tail, held, others, theirs, zrecv, recv, send, lrecv, lsend, sibrecv, osem, local):
    grp, sub = lax.axis_index("grp"), lax.axis_index("sub")
    zh, core = grp // 2, lax.rem(grp, 2)
    x, zl, y = sub // 8, lax.rem(sub // 4, 2), lax.rem(sub, 4)

    def device(x, y, zh, zl, core):
        return (zh * 2 + core, x * 8 + zl * 4 + y)

    xr, xl, yr, yl = lax.rem(x + 1, 4), lax.rem(x + 3, 4), lax.rem(y + 1, 4), lax.rem(y + 3, 4)
    x_right, x_left = device(xr, y, zh, zl, core), device(xl, y, zh, zl, core)
    y_right, y_left = device(x, yr, zh, zl, core), device(x, yl, zh, zl, core)
    mate = device(x, y, zh, 1 - zl, core)
    cross = device(x, y, 1 - zh, 1 - zl, core)
    sibling = device(x, y, zh, zl, 1 - core)
    around = (x_right, x_left, y_right, y_left, mate, cross, sibling)

    rows = (own, others)

    def chunk(i):
        return held.at[i] if i < NC - LAST else tail.at[i - (NC - LAST)]

    barrier = pltpu.get_barrier_semaphore()
    for other in around:
        pl.semaphore_signal(barrier, inc=1, device_id=other, device_id_type=MESH)

    def column(i, side):
        if i < NS:
            return pl.multiple_of(side * (NS * W) + i * W, 128)
        return (NS + i) * W

    def kcols(g):
        return pl.ds(pl.multiple_of(g * KL, 128), KL)

    def go(src, dst, ssem, rsem, to):
        pltpu.make_async_remote_copy(src, dst, ssem, rsem, device_id=to, device_id_type=MESH).start()

    def wait(like, sem):
        pltpu.make_async_copy(like, like, sem).wait()

    for i in range(NC):
        pltpu.make_async_copy(right.at[:, pl.ds(column(i, zl), W)], chunk(i).at[x, zl, y], local.at[0]).start()
    mine = pltpu.make_async_copy(left, own.at[:, kcols(grp)], local.at[1])
    mine.start()
    with jax.named_scope("barrier"):
        pl.semaphore_wait(barrier, len(around))

    here_k, other_k = kcols(grp), kcols((1 - zh) * 2 + core)
    some = NC // 2
    a_part = own.at[pl.ds(0, M // PARTS), pl.ds(0, KL)]
    two_blocks, three_blocks = own.at[:, pl.ds(0, 2 * KL)], own.at[:, pl.ds(0, 3 * KL)]

    def exchange(i):
        src = right.at[:, pl.ds(column(i, 1 - zl), W)]
        go(src, chunk(i).at[x, zl, y], send.at[0], zrecv.at[i], mate)

    def part(j):
        return pl.ds(j * (M // PARTS), M // PARTS)

    def left_first(j):
        go(left.at[part(j)], others.at[part(j), here_k], lsend.at[0], lrecv.at[0, j], mate)
        go(left.at[part(j)], others.at[part(j), here_k], lsend.at[0], lrecv.at[1, j], cross)
        go(left.at[part(j)], own.at[part(j), here_k], lsend.at[0], sibrecv.at[1], sibling)

    def left_mate(j):
        wait(a_part, lrecv.at[0, j])
        block = others.at[part(j), here_k]
        go(block, own.at[part(j), here_k], lsend.at[0], lrecv.at[2, j], cross)
        go(block, block, lsend.at[1], sibrecv.at[0], sibling)
        wait(a_part, lrecv.at[1, j])
        block = others.at[part(j), other_k]
        go(block, block, lsend.at[1], sibrecv.at[0], sibling)

    def left_own(j):
        wait(a_part, lrecv.at[2, j])
        block = own.at[part(j), other_k]
        go(block, block, lsend.at[1], sibrecv.at[1], sibling)

    def arrived(i, k):
        like = (None, held.at[0, 0, 0], held.at[0, 0, :, 0], held.at[0, 0], held.at[0, :, 0])[k]
        wait(like, recv.at[i, k - 1])

    def piece(i, along, a, b, z):
        return chunk(i).at[a, z, b] if along == 0 else chunk(i).at[b, z, a]

    def both(i, k, up, down, to):
        go(up, up, send.at[k], recv.at[i, k - 1], to[0])
        go(down, down, send.at[k], recv.at[i, k - 1], to[1])

    def stage(i, k):
        first = i % 2
        along = first if k < 3 else 1 - first
        here, lo, hi = ((x, xl, xr), (y, yl, yr))[along]
        fixed = (y, x)[along] if k < 3 else slice(None)
        to = ((x_right, x_left), (y_right, y_left))[along]
        if k == 0:
            src, dst = right.at[:, pl.ds(column(i, zl), W)], chunk(i).at[x, zl, y]
            go(src, dst, send.at[1], recv.at[i, 0], to[0])
            go(src, dst, send.at[1], recv.at[i, 0], to[1])
        elif k == 1:
            wait(held.at[0, 0, 0, 0], zrecv.at[i])
            block = chunk(i).at[x, 1 - zl, y]
            both(i, 1, block, block, to)
        else:
            arrived(i, k - 1)
            if k == 3:
                low, high = piece(i, along, here, fixed, 0), piece(i, along, here, fixed, 1)
                both(i, 3, low, high, to)
                go(high, high, send.at[3], recv.at[i, 3], to[0])
                go(low, low, send.at[3], recv.at[i, 3], to[1])
            else:
                both(i, k, piece(i, along, lo, fixed, 0), piece(i, along, hi, fixed, 1), to)

    def multiply(side, i, write):
        block = chunk(i)

        @pl.loop(0, M // TILE, unroll=M // TILE)
        def _(t):
            at = pl.ds(pl.multiple_of(t * TILE, TILE), TILE)
            value = jnp.dot(rows[side][at, :], block[...].reshape(K, W), preferred_element_type=jnp.float32)
            write(at, value.astype(jnp.bfloat16))

    def compute_mate(i):
        def write(at, value):
            theirs[i, at, :] = value

        multiply(MATE, i, write)
        go(theirs.at[i], out.at[:, pl.ds(column(i, zl), W)], osem.at[0], osem.at[1], mate)

    def compute_own(i):
        c = column(i, zl)

        def write(at, value):
            out[at, pl.ds(c, W)] = value

        multiply(OWN, i, write)

    met = set()

    def once(what):
        new = what not in met
        met.add(what)
        return new

    def full(i):
        if once(("full", i)):
            with jax.named_scope(f"w4_{i}"):
                arrived(i, 4)

    for op, i in ORDER:
        if op == 3 and once("local"):
            wait(held.at[pl.ds(0, some), 0, :, 0], local.at[0])
        if op in ("m", "o", "f"):
            full(i)
        if op == "m" and once("mate"):
            with jax.named_scope("wmate"):
                wait(two_blocks, sibrecv.at[0])
        if op == "o" and once("own"):
            with jax.named_scope("wown"):
                wait(two_blocks, sibrecv.at[1])
                mine.wait()
        with jax.named_scope(f"{op}_{i}"):
            if op == "z":
                exchange(i)
            elif op == "p":
                stage(i, 0)
            elif op == "L":
                left_first(i)
            elif op == "LM":
                left_mate(i)
            elif op == "LO":
                left_own(i)
            elif op == "m":
                compute_mate(i)
            elif op == "o":
                compute_own(i)
            elif op != "f":
                stage(i, op)

    with jax.named_scope("sends"):
        for k, like in enumerate((
            held.at[pl.ds(0, some), 0, :, 0],
            held.at[pl.ds(0, some), 0],
            held.at[pl.ds(0, some), 0, 0],
            held.at[pl.ds(0, some)],
            held.at[pl.ds(0, some), :, 0],
        )):
            wait(like, send.at[k])
        wait(own, lsend.at[0])
        wait(three_blocks, lsend.at[1])
    with jax.named_scope("outs"):
        wait(theirs, osem.at[0])
        wait(theirs, osem.at[1])


def finish(done, own, tail, out, last, sems):
    copies = []
    for b in range(BLOCKS):
        at = pl.ds(b * (M // BLOCKS), M // BLOCKS)
        copies.append(pltpu.make_async_copy(done.at[at], out.at[at, pl.ds(0, NA)], sems.at[b]))
        copies[-1].start()
    for j in range(LAST):

        @pl.loop(0, M // TILE, unroll=M // TILE)
        def _(t):
            at = pl.ds(pl.multiple_of(t * TILE, TILE), TILE)
            value = jnp.dot(own[at, :], tail[j].reshape(K, W), preferred_element_type=jnp.float32)
            last[j, at, :] = value.astype(jnp.bfloat16)

        copies.append(pltpu.make_async_copy(last.at[j], out.at[:, pl.ds(NA + j * W, W)], sems.at[BLOCKS + j]))
        copies[-1].start()
    for copy in copies:
        copy.wait()


BLOCKS = 4


def shards(left, right):
    chunks = (4, 2, 4, DEPTH, W)
    done, own, tail = pl.pallas_call(
        gather,
        out_shape=(
            pltpu.VMEM((M, NA), jnp.bfloat16),
            pltpu.VMEM((M, K), jnp.bfloat16),
            pltpu.VMEM((LAST,) + chunks, jnp.bfloat16),
        ),
        in_specs=[pl.BlockSpec(memory_space=pltpu.HBM)] * 2,
        out_specs=(pl.BlockSpec(memory_space=pltpu.VMEM),) * 3,
        scratch_shapes=[
            pltpu.VMEM((NC - LAST,) + chunks, jnp.bfloat16),
            pltpu.VMEM((M, K), jnp.bfloat16),
            pltpu.VMEM((NS, M, W), jnp.bfloat16),
            pltpu.SemaphoreType.DMA((NC,)),
            pltpu.SemaphoreType.DMA((NC, 4)),
            pltpu.SemaphoreType.DMA((5,)),
            pltpu.SemaphoreType.DMA((3, PARTS)),
            pltpu.SemaphoreType.DMA((2,)),
            pltpu.SemaphoreType.DMA((2,)),
            pltpu.SemaphoreType.DMA((2,)),
            pltpu.SemaphoreType.DMA((2,)),
        ],
        compiler_params=pltpu.CompilerParams(
            collective_id=0, has_side_effects=True, vmem_limit_bytes=GRANT
        ),
        cost_estimate=pl.CostEstimate(flops=2 * M * NA * K, bytes_accessed=2 * M * N, transcendentals=0),
    )(left, right)
    return pl.pallas_call(
        finish,
        out_shape=jax.ShapeDtypeStruct((M, N), jnp.bfloat16),
        in_specs=[pl.BlockSpec(memory_space=pltpu.VMEM)] * 3,
        out_specs=pl.BlockSpec(memory_space=pltpu.HBM),
        scratch_shapes=[pltpu.VMEM((LAST, M, W), jnp.bfloat16), pltpu.SemaphoreType.DMA((BLOCKS + LAST,))],
        compiler_params=pltpu.CompilerParams(vmem_limit_bytes=16 * 2**20),
        cost_estimate=pl.CostEstimate(flops=2 * M * LAST * W * K, bytes_accessed=4 * M * N, transcendentals=0),
    )(done, own, tail)


GRANT = 48 * 2**20


def solution(mesh):
    placed = (P("sub", "grp"), P("sub", "grp"))
    return jax.shard_map(
        shards, mesh=mesh, in_specs=placed, out_specs=P("sub", "grp"), check_vma=False
    )
```

```python
import jax
import jax.numpy as jnp
from jax import lax
from jax.experimental import pallas as pl
from jax.experimental.pallas import tpu as pltpu
from jax.sharding import PartitionSpec as P

MESH = pl.DeviceIdType.MESH
M, N, K, DEPTH, KL = 768, 6144, 1536, 48, 384
W = 256
NS = 6
ND = N // W - 2 * NS
NC = NS + ND
LAST = 2
NA = N - LAST * W
TILE = 256
PARTS = 3
OWN, MATE = 0, 1

NAMES = {
    "z": "exchange_z", "p": "send_own_rows", 1: "send_pair_rows", 2: "send_first_axis", 3: "send_blocks", 4: "send_second_axis",
    "m": "product_mate", "o": "product_own", "f": "chunk_whole", "L": "left_first", "LM": "left_mate", "LO": "left_own",
}

ORDER = (
    ("z", 4), ("z", 1), ("z", 9), ("p", 4), ("p", 9), ("z", 12), ("z", 5), ("p", 14),
    ("z", 3), ("p", 15), ("z", 16), ("p", 13), ("z", 15), ("p", 11), ("p", 2), ("z", 14),
    ("p", 1), ("z", 2), ("z", 0), ("L", 1), ("p", 10), ("L", 0), ("L", 2), (1, 4),
    (1, 1), ("p", 0), (1, 9), (1, 12), ("z", 6), ("p", 12), (1, 5), ("p", 5),
    ("p", 16), ("z", 13), ("p", 7), (1, 16), (1, 15), (2, 4), ("p", 8), ("z", 11),
    (1, 14), ("p", 6), (2, 1), ("z", 10), ("p", 17), (1, 0), ("p", 3), (1, 3),
    (2, 5), (1, 2), (2, 12), (2, 9), ("z", 7), (2, 16), (3, 4), (3, 1),
    (2, 15), (2, 3), (2, 2), (2, 14), ("LM", 1), (4, 4), (3, 5), (4, 1),
    (3, 12), ("LM", 0), ("z", 17), ("LM", 2), ("z", 8), (3, 2), (3, 3), (2, 0),
    (1, 11), (1, 6), (3, 14), (3, 9), ("m", 4), (4, 5), (4, 3), (1, 10),
    (1, 7), (4, 12), (1, 8), ("m", 1), (3, 0), ("LO", 2), ("LO", 0), (3, 15),
    ("LO", 1), (1, 13), (1, 17), (2, 7), (2, 11), (4, 2), ("m", 3), (4, 14),
    (2, 8), (2, 6), (4, 0), (4, 9), (3, 7), (3, 6), (2, 13), (3, 11),
    (2, 17), ("m", 2), ("m", 0), ("m", 5), (3, 8), (4, 15), (2, 10), ("o", 2),
    (4, 6), ("o", 9), ("o", 0), (3, 13), ("o", 5), (4, 11), ("o", 3), ("o", 14),
    (4, 7), (4, 8), (3, 10), (3, 16), (3, 17), ("o", 12), ("o", 1), (4, 13),
    ("o", 4), (4, 10), ("o", 11), ("o", 8), ("o", 15), ("o", 6), (4, 17), (4, 16),
    ("o", 7), ("o", 10), ("o", 13), ("f", 17), ("f", 16),
)


def gather(left, right, out, own, tail, held, others, theirs, zrecv, recv, send, lrecv, lsend, sibrecv, osem, local):
    grp, sub = lax.axis_index("grp"), lax.axis_index("sub")
    zh, core = grp // 2, lax.rem(grp, 2)
    x, zl, y = sub // 8, lax.rem(sub // 4, 2), lax.rem(sub, 4)

    def device(x, y, zh, zl, core):
        return (zh * 2 + core, x * 8 + zl * 4 + y)

    xr, xl, yr, yl = lax.rem(x + 1, 4), lax.rem(x + 3, 4), lax.rem(y + 1, 4), lax.rem(y + 3, 4)
    x_right, x_left = device(xr, y, zh, zl, core), device(xl, y, zh, zl, core)
    y_right, y_left = device(x, yr, zh, zl, core), device(x, yl, zh, zl, core)
    mate = device(x, y, zh, 1 - zl, core)
    cross = device(x, y, 1 - zh, 1 - zl, core)
    sibling = device(x, y, zh, zl, 1 - core)
    around = (x_right, x_left, y_right, y_left, mate, cross, sibling)

    rows = (own, others)

    def chunk(i):
        return held.at[i] if i < NC - LAST else tail.at[i - (NC - LAST)]

    barrier = pltpu.get_barrier_semaphore()
    for other in around:
        pl.semaphore_signal(barrier, inc=1, device_id=other, device_id_type=MESH)

    def column(i, side):
        if i < NS:
            return pl.multiple_of(side * (NS * W) + i * W, 128)
        return (NS + i) * W

    def kcols(g):
        return pl.ds(pl.multiple_of(g * KL, 128), KL)

    def go(src, dst, ssem, rsem, to):
        pltpu.make_async_remote_copy(src, dst, ssem, rsem, device_id=to, device_id_type=MESH).start()

    def wait(like, sem):
        pltpu.make_async_copy(like, like, sem).wait()

    for i in range(NC):
        pltpu.make_async_copy(right.at[:, pl.ds(column(i, zl), W)], chunk(i).at[x, zl, y], local.at[0]).start()
    mine = pltpu.make_async_copy(left, own.at[:, kcols(grp)], local.at[1])
    mine.start()
    with jax.named_scope("barrier"):
        pl.semaphore_wait(barrier, len(around))

    here_k, other_k = kcols(grp), kcols((1 - zh) * 2 + core)
    some = NC // 2
    a_part = own.at[pl.ds(0, M // PARTS), pl.ds(0, KL)]
    two_blocks, three_blocks = own.at[:, pl.ds(0, 2 * KL)], own.at[:, pl.ds(0, 3 * KL)]

    def exchange(i):
        src = right.at[:, pl.ds(column(i, 1 - zl), W)]
        go(src, chunk(i).at[x, zl, y], send.at[0], zrecv.at[i], mate)

    def part(j):
        return pl.ds(j * (M // PARTS), M // PARTS)

    def left_first(j):
        go(left.at[part(j)], others.at[part(j), here_k], lsend.at[0], lrecv.at[0, j], mate)
        go(left.at[part(j)], others.at[part(j), here_k], lsend.at[0], lrecv.at[1, j], cross)
        go(left.at[part(j)], own.at[part(j), here_k], lsend.at[0], sibrecv.at[1], sibling)

    def left_mate(j):
        wait(a_part, lrecv.at[0, j])
        block = others.at[part(j), here_k]
        go(block, own.at[part(j), here_k], lsend.at[0], lrecv.at[2, j], cross)
        go(block, block, lsend.at[1], sibrecv.at[0], sibling)
        wait(a_part, lrecv.at[1, j])
        block = others.at[part(j), other_k]
        go(block, block, lsend.at[1], sibrecv.at[0], sibling)

    def left_own(j):
        wait(a_part, lrecv.at[2, j])
        block = own.at[part(j), other_k]
        go(block, block, lsend.at[1], sibrecv.at[1], sibling)

    def arrived(i, k):
        like = (None, held.at[0, 0, 0], held.at[0, 0, :, 0], held.at[0, 0], held.at[0, :, 0])[k]
        wait(like, recv.at[i, k - 1])

    def piece(i, along, a, b, z):
        return chunk(i).at[a, z, b] if along == 0 else chunk(i).at[b, z, a]

    def both(i, k, up, down, to):
        go(up, up, send.at[k], recv.at[i, k - 1], to[0])
        go(down, down, send.at[k], recv.at[i, k - 1], to[1])

    def stage(i, k):
        first = i % 2
        along = first if k < 3 else 1 - first
        here, lo, hi = ((x, xl, xr), (y, yl, yr))[along]
        fixed = (y, x)[along] if k < 3 else slice(None)
        to = ((x_right, x_left), (y_right, y_left))[along]
        if k == 0:
            src, dst = right.at[:, pl.ds(column(i, zl), W)], chunk(i).at[x, zl, y]
            go(src, dst, send.at[1], recv.at[i, 0], to[0])
            go(src, dst, send.at[1], recv.at[i, 0], to[1])
        elif k == 1:
            wait(held.at[0, 0, 0, 0], zrecv.at[i])
            block = chunk(i).at[x, 1 - zl, y]
            both(i, 1, block, block, to)
        else:
            arrived(i, k - 1)
            if k == 3:
                low, high = piece(i, along, here, fixed, 0), piece(i, along, here, fixed, 1)
                both(i, 3, low, high, to)
                go(high, high, send.at[3], recv.at[i, 3], to[0])
                go(low, low, send.at[3], recv.at[i, 3], to[1])
            else:
                both(i, k, piece(i, along, lo, fixed, 0), piece(i, along, hi, fixed, 1), to)

    def multiply(side, i, write):
        block = chunk(i)

        @pl.loop(0, M // TILE, unroll=M // TILE)
        def _(t):
            at = pl.ds(pl.multiple_of(t * TILE, TILE), TILE)
            value = jnp.dot(rows[side][at, :], block[...].reshape(K, W), preferred_element_type=jnp.float32)
            write(at, value.astype(jnp.bfloat16))

    def compute_mate(i):
        def write(at, value):
            theirs[i, at, :] = value

        multiply(MATE, i, write)
        go(theirs.at[i], out.at[:, pl.ds(column(i, zl), W)], osem.at[0], osem.at[1], mate)

    def compute_own(i):
        c = column(i, zl)

        def write(at, value):
            out[at, pl.ds(c, W)] = value

        multiply(OWN, i, write)

    met = set()

    def once(what):
        new = what not in met
        met.add(what)
        return new

    def full(i):
        if once(("full", i)):
            with jax.named_scope("wait_chunk"):
                arrived(i, 4)

    for op, i in ORDER:
        if op == 3 and once("local"):
            wait(held.at[pl.ds(0, some), 0, :, 0], local.at[0])
        if op in ("m", "o", "f"):
            full(i)
        if op == "m" and once("mate"):
            with jax.named_scope("wait_left_mate"):
                wait(two_blocks, sibrecv.at[0])
        if op == "o" and once("own"):
            with jax.named_scope("wait_left_own"):
                wait(two_blocks, sibrecv.at[1])
                mine.wait()
        with jax.named_scope(NAMES[op]):
            if op == "z":
                exchange(i)
            elif op == "p":
                stage(i, 0)
            elif op == "L":
                left_first(i)
            elif op == "LM":
                left_mate(i)
            elif op == "LO":
                left_own(i)
            elif op == "m":
                compute_mate(i)
            elif op == "o":
                compute_own(i)
            elif op != "f":
                stage(i, op)

    with jax.named_scope("wait_sends"):
        for k, like in enumerate((
            held.at[pl.ds(0, some), 0, :, 0],
            held.at[pl.ds(0, some), 0],
            held.at[pl.ds(0, some), 0, 0],
            held.at[pl.ds(0, some)],
            held.at[pl.ds(0, some), :, 0],
        )):
            wait(like, send.at[k])
        wait(own, lsend.at[0])
        wait(three_blocks, lsend.at[1])
    with jax.named_scope("wait_products"):
        wait(theirs, osem.at[0])
        wait(theirs, osem.at[1])


def finish(done, own, tail, out, last, sems):
    copies = []
    for b in range(BLOCKS):
        at = pl.ds(b * (M // BLOCKS), M // BLOCKS)
        copies.append(pltpu.make_async_copy(done.at[at], out.at[at, pl.ds(0, NA)], sems.at[b]))
        copies[-1].start()
    for j in range(LAST):

        @pl.loop(0, M // TILE, unroll=M // TILE)
        def _(t):
            at = pl.ds(pl.multiple_of(t * TILE, TILE), TILE)
            value = jnp.dot(own[at, :], tail[j].reshape(K, W), preferred_element_type=jnp.float32)
            last[j, at, :] = value.astype(jnp.bfloat16)

        copies.append(pltpu.make_async_copy(last.at[j], out.at[:, pl.ds(NA + j * W, W)], sems.at[BLOCKS + j]))
        copies[-1].start()
    for copy in copies:
        copy.wait()


BLOCKS = 4


def shards(left, right):
    chunks = (4, 2, 4, DEPTH, W)
    done, own, tail = pl.pallas_call(
        gather,
        out_shape=(
            pltpu.VMEM((M, NA), jnp.bfloat16),
            pltpu.VMEM((M, K), jnp.bfloat16),
            pltpu.VMEM((LAST,) + chunks, jnp.bfloat16),
        ),
        in_specs=[pl.BlockSpec(memory_space=pltpu.HBM)] * 2,
        out_specs=(pl.BlockSpec(memory_space=pltpu.VMEM),) * 3,
        scratch_shapes=[
            pltpu.VMEM((NC - LAST,) + chunks, jnp.bfloat16),
            pltpu.VMEM((M, K), jnp.bfloat16),
            pltpu.VMEM((NS, M, W), jnp.bfloat16),
            pltpu.SemaphoreType.DMA((NC,)),
            pltpu.SemaphoreType.DMA((NC, 4)),
            pltpu.SemaphoreType.DMA((5,)),
            pltpu.SemaphoreType.DMA((3, PARTS)),
            pltpu.SemaphoreType.DMA((2,)),
            pltpu.SemaphoreType.DMA((2,)),
            pltpu.SemaphoreType.DMA((2,)),
            pltpu.SemaphoreType.DMA((2,)),
        ],
        compiler_params=pltpu.CompilerParams(
            collective_id=0, has_side_effects=True, vmem_limit_bytes=GRANT
        ),
        cost_estimate=pl.CostEstimate(flops=2 * M * NA * K, bytes_accessed=2 * M * N, transcendentals=0),
    )(left, right)
    return pl.pallas_call(
        finish,
        out_shape=jax.ShapeDtypeStruct((M, N), jnp.bfloat16),
        in_specs=[pl.BlockSpec(memory_space=pltpu.VMEM)] * 3,
        out_specs=pl.BlockSpec(memory_space=pltpu.HBM),
        scratch_shapes=[pltpu.VMEM((LAST, M, W), jnp.bfloat16), pltpu.SemaphoreType.DMA((BLOCKS + LAST,))],
        compiler_params=pltpu.CompilerParams(vmem_limit_bytes=16 * 2**20),
        cost_estimate=pl.CostEstimate(flops=2 * M * LAST * W * K, bytes_accessed=4 * M * N, transcendentals=0),
    )(done, own, tail)


GRANT = 48 * 2**20


def solution(mesh):
    placed = (P("sub", "grp"), P("sub", "grp"))
    return jax.shard_map(
        shards, mesh=mesh, in_specs=placed, out_specs=P("sub", "grp"), check_vma=False
    )
```
